32 devices in a mesh: row: 4 (over y, core), col: 8 (over z, x).
Axes of the slice: x: 2, y: 2, z: 4, core: 2. Of those that a mesh axis runs over, the one named last changes fastest.
Arguments:
- probes: bfloat16 [512, 16384], P(None, ('row', 'col')), may hold values from -6 to 6
- own_blocks: bfloat16 [3, 16384, 512], P(None, ('row', 'col')), may hold values from -0.1875 to 0.1875
- cross_blocks: bfloat16 [3, 16384, 512], P(None, ('row', 'col')), may hold values from -0.1875 to 0.1875
- level_perm: int32 [3, 16384], P(None, ('row', 'col')), may hold values from 0 to 511, as said below
Outputs:
- mixed: bfloat16 [512, 16384], P(None, ('row', 'col'))
The draws below stay inside these ranges and needn't reach their ends.
Inputs may be any that keep to these rules, and one draw needn't show every extreme that they name: `level_perm`: each aligned run of 512 entries of a level is a permutation of 0 to 511.
All inputs are finite; a program needn't handle non-finite values.
Results may differ from the reference program's by a relative error of at most 0.0057.
Values may be sent and summed in bfloat16 or wider, within the bound.
A program may use at most 64 MiB of HBM per device.

```python
import jax
import jax.numpy as jnp
from jax import lax

BR = 512
PROBES = 512
LEVELS = 3
BLOCKS = 32
NK = 16384
N_ROW = 4
N_COL = 8


def draw_level_perm(key, part):
    keys = jax.random.split(jax.random.fold_in(key, 17), LEVELS * BLOCKS)
    perms = jax.vmap(lambda k: jax.random.permutation(k, BR))(keys)
    return perms.reshape(LEVELS, BLOCKS * BR).astype(jnp.int32)


def steps_of(rng, extent, cuts, least, top_value):
    factor_of = 1.0
    for dim, blocks in cuts:
        draws = jax.random.uniform(jax.random.fold_in(jax.random.fold_in(rng, 6), dim), (blocks,), jnp.float32, least / len(cuts), top_value / len(cuts))
        factor_of = factor_of * jnp.repeat(jnp.exp(draws), extent[dim] // blocks).reshape((-1,) + (1,) * (len(extent) - 1 - dim))
    return factor_of


def bell_draw(own_key, extent, spread, bound, cuts=(), kind=jnp.bfloat16):
    array = jax.random.normal(own_key, extent, jnp.float32) * spread
    if len(cuts) > 0:
        array = steps_of(own_key, extent, cuts, -0.22, 0.18) * array
    return jnp.clip(array, min=-bound, max=bound).astype(kind)


def setup_inputs(seed: int = 0) -> dict:
    streams_of = jax.random.split(jax.random.key(seed), 5)
    probes = bell_draw(streams_of[0], (PROBES, NK), 1.0, 6.0, ((1, 32),))
    own_blocks = bell_draw(streams_of[1], (LEVELS, NK, BR), (2 * BR) ** -0.5, 0.1875, ((1, 32),))
    cross_blocks = bell_draw(streams_of[2], (LEVELS, NK, BR), (2 * BR) ** -0.5, 0.1875, ((1, 32),))
    level_perm = draw_level_perm(jax.random.fold_in(streams_of[4], 71), 0)
    return {"probes": probes, "own_blocks": own_blocks, "cross_blocks": cross_blocks, "level_perm": level_perm}


def reference(probes, own_blocks, cross_blocks, level_perm):
    ncol_bits = N_COL.bit_length() - 1
    nrow_bits = N_ROW.bit_length() - 1
    bits = [ncol_bits - 1, ncol_bits + nrow_bits - 1, 0]
    panel = probes.reshape(PROBES, BLOCKS, BR).transpose(1, 0, 2)
    index = jnp.arange(BLOCKS, dtype=jnp.int32)
    for level in range(LEVELS):
        partner_index = jnp.bitwise_xor(index, jnp.int32(1 << bits[level]))
        partner = panel[partner_index]
        own = own_blocks[level].reshape(BLOCKS, BR, BR)
        cross = cross_blocks[level].reshape(BLOCKS, BR, BR)
        order = level_perm[level].reshape(BLOCKS, BR)

        def one_block(items):
            mine, other, own_b, cross_b, order_b = items
            total = jnp.dot(mine, own_b, preferred_element_type=jnp.float32)
            total = total + jnp.dot(other, cross_b, preferred_element_type=jnp.float32)
            return jnp.take(total, order_b, axis=1).astype(jnp.bfloat16)

        panel = lax.map(one_block, (panel, partner, own, cross, order))
    return panel.transpose(1, 0, 2).reshape(PROBES, NK)
```

```python
import functools

import jax
import jax.numpy as jnp
from jax import lax
from jax.experimental import pallas as pl
from jax.experimental.pallas import tpu as pltpu
from jax.sharding import PartitionSpec as P

LEVELS = 3
BODY = 64
TAIL = (48, 32, 32, 16)


def row_chunks(rows):
    sizes = list(TAIL) if rows > sum(TAIL) else []
    left = rows - sum(sizes)
    head = [BODY] * (left // BODY)
    if left % BODY:
        head.append(left % BODY)
    chunks, start = [], 0
    for size in head + sizes:
        chunks.append((start, size))
        start += size
    return chunks


def flip(index, distance):
    return index + distance - 2 * distance * lax.rem(lax.div(index, distance), 2)


def kernel(
    n_row, n_col, chunks,
    probes, own, cross, perm,
    out,
    mine, own_v, cross_v, perm_v, own_p, cross_p, panels, others,
    load_sem, perm_sem, send_sem, recv_sem,
):
    row, col = lax.axis_index("row"), lax.axis_index("col")
    partners = [
        (row, flip(col, n_col // 2)),
        (flip(row, n_row // 2), col),
        (row, flip(col, 1)),
    ]
    barrier = pltpu.get_barrier_semaphore()
    for partner in partners:
        pl.semaphore_signal(
            barrier, inc=1, device_id=partner, device_id_type=pl.DeviceIdType.MESH
        )
    loads = [
        pltpu.make_async_copy(perm, perm_v, perm_sem),
        pltpu.make_async_copy(own, own_v, load_sem.at[0]),
        pltpu.make_async_copy(cross, cross_v, load_sem.at[1]),
        pltpu.make_async_copy(probes, mine, load_sem.at[2]),
    ]
    for load in loads:
        load.start()
    pl.semaphore_wait(barrier, LEVELS)

    def send(level, k):
        start, size = chunks[k]
        rows = pl.ds(start, size)
        source = probes.at[rows] if level == 0 else panels.at[level - 1, rows]
        return pltpu.make_async_remote_copy(
            src_ref=source,
            dst_ref=others.at[level, rows],
            send_sem=send_sem.at[level, k],
            recv_sem=recv_sem.at[level, k],
            device_id=partners[level],
            device_id_type=pl.DeviceIdType.MESH,
        )

    copies = {}
    for k in range(len(chunks)):
        copies[0, k] = send(0, k)
        copies[0, k].start()

    for load in loads:
        load.wait()
    depth = own.shape[1]
    for level in range(LEVELS):
        index = lax.broadcasted_iota(jnp.int32, (depth, depth), 0)
        pick = jnp.where(index == perm_v[level : level + 1, :], 1.0, 0.0).astype(jnp.bfloat16)
        for source, target in ((own_v, own_p), (cross_v, cross_p)):
            moved = jnp.dot(source[level], pick, preferred_element_type=jnp.float32)
            target[level] = moved.astype(jnp.bfloat16)

    def step(level, k):
        start, size = chunks[k]
        rows = pl.ds(start, size)
        held = mine[rows] if level == 0 else panels[level - 1, rows]
        total = jnp.dot(held, own_p[level], preferred_element_type=jnp.float32)
        copies[level, k].wait_recv()
        total += jnp.dot(others[level, rows], cross_p[level], preferred_element_type=jnp.float32)
        result = total.astype(jnp.bfloat16)
        if level < LEVELS - 1:
            panels[level, rows] = result
            copies[level + 1, k] = send(level + 1, k)
            copies[level + 1, k].start()
        else:
            out[rows] = result

    for k in range(len(chunks) + LEVELS - 1):
        for level in range(LEVELS):
            if 0 <= k - level < len(chunks):
                step(level, k - level)
    for copy in copies.values():
        copy.wait_send()


def per_device(n_row, n_col, probes, own_blocks, cross_blocks, level_perm):
    rows, depth = probes.shape
    chunks = row_chunks(rows)
    weights = pltpu.VMEM(own_blocks.shape, jnp.bfloat16)
    return pl.pallas_call(
        functools.partial(kernel, n_row, n_col, chunks),
        out_shape=jax.ShapeDtypeStruct((rows, depth), jnp.bfloat16),
        in_specs=[pl.BlockSpec(memory_space=pltpu.HBM)] * 4,
        out_specs=pl.BlockSpec(memory_space=pltpu.VMEM),
        scratch_shapes=[
            pltpu.VMEM((rows, depth), jnp.bfloat16),
            weights,
            weights,
            pltpu.VMEM(level_perm.shape, jnp.int32),
            weights,
            weights,
            pltpu.VMEM((LEVELS - 1, rows, depth), jnp.bfloat16),
            pltpu.VMEM((LEVELS, rows, depth), jnp.bfloat16),
            pltpu.SemaphoreType.DMA((3,)),
            pltpu.SemaphoreType.DMA,
            pltpu.SemaphoreType.DMA((LEVELS, len(chunks))),
            pltpu.SemaphoreType.DMA((LEVELS, len(chunks))),
        ],
        compiler_params=pltpu.CompilerParams(
            collective_id=0, has_side_effects=True, vmem_limit_bytes=60 * 2**20
        ),
        cost_estimate=pl.CostEstimate(
            flops=24 * rows * depth * depth, bytes_accessed=8 * rows * depth * 2, transcendentals=0
        ),
    )(probes, own_blocks, cross_blocks, level_perm)


def solution(mesh):
    n_row, n_col = mesh.shape["row"], mesh.shape["col"]
    placed = (
        P(None, ("row", "col")),
        P(None, ("row", "col"), None),
        P(None, ("row", "col"), None),
        P(None, ("row", "col")),
    )
    return jax.shard_map(
        functools.partial(per_device, n_row, n_col),
        mesh=mesh,
        in_specs=placed,
        out_specs=P(None, ("row", "col")),
        check_vma=False,
    )
```

```python
import functools

import jax
import jax.numpy as jnp
from jax import lax
from jax.experimental import pallas as pl
from jax.experimental.pallas import tpu as pltpu
from jax.sharding import PartitionSpec as P

LEVELS = 3
BODY = 32
TAIL = (16, 16)
AHEAD = 3


def row_chunks(rows):
    sizes = list(TAIL) if rows > sum(TAIL) else []
    left = rows - sum(sizes)
    head = [BODY] * (left // BODY)
    if left % BODY:
        head.append(left % BODY)
    chunks, start = [], 0
    for size in head + sizes:
        chunks.append((start, size))
        start += size
    return chunks


def flip(index, distance):
    return index + distance - 2 * distance * lax.rem(lax.div(index, distance), 2)


def kernel(
    n_row, n_col, chunks,
    probes, own, cross, perm,
    out,
    mine, own_v, cross_v, perm_v, own_p, cross_p, panels, others,
    load_sem, perm_sem, send_sem, recv_sem,
):
    row, col = lax.axis_index("row"), lax.axis_index("col")
    partners = [
        (row, flip(col, n_col // 2)),
        (flip(row, n_row // 2), col),
        (row, flip(col, 1)),
    ]
    barrier = pltpu.get_barrier_semaphore()
    for partner in partners:
        pl.semaphore_signal(
            barrier, inc=1, device_id=partner, device_id_type=pl.DeviceIdType.MESH
        )
    loads = [
        pltpu.make_async_copy(perm, perm_v, perm_sem),
        pltpu.make_async_copy(own, own_v, load_sem.at[0]),
        pltpu.make_async_copy(cross, cross_v, load_sem.at[1]),
        pltpu.make_async_copy(probes, mine, load_sem.at[2]),
    ]
    for load in loads:
        load.start()
    pl.semaphore_wait(barrier, LEVELS)

    def send(level, k):
        start, size = chunks[k]
        rows = pl.ds(start, size)
        source = probes.at[rows] if level == 0 else panels.at[level - 1, rows]
        return pltpu.make_async_remote_copy(
            src_ref=source,
            dst_ref=others.at[level, rows],
            send_sem=send_sem.at[level, k],
            recv_sem=recv_sem.at[level, k],
            device_id=partners[level],
            device_id_type=pl.DeviceIdType.MESH,
        )

    copies = {}
    for k in range(min(AHEAD, len(chunks))):
        copies[0, k] = send(0, k)
        copies[0, k].start()

    for load in loads:
        load.wait()
    depth = own.shape[1]
    for level in range(LEVELS):
        index = lax.broadcasted_iota(jnp.int32, (depth, depth), 0)
        pick = jnp.where(index == perm_v[level : level + 1, :], 1.0, 0.0).astype(jnp.bfloat16)
        for source, target in ((own_v, own_p), (cross_v, cross_p)):
            moved = jnp.dot(source[level], pick, preferred_element_type=jnp.float32)
            target[level] = moved.astype(jnp.bfloat16)

    def step(level, k):
        start, size = chunks[k]
        rows = pl.ds(start, size)
        held = mine[rows] if level == 0 else panels[level - 1, rows]
        total = jnp.dot(held, own_p[level], preferred_element_type=jnp.float32)
        copies[level, k].wait_recv()
        if level == 0 and k + AHEAD < len(chunks):
            copies[0, k + AHEAD] = send(0, k + AHEAD)
            copies[0, k + AHEAD].start()
        total += jnp.dot(others[level, rows], cross_p[level], preferred_element_type=jnp.float32)
        result = total.astype(jnp.bfloat16)
        if level < LEVELS - 1:
            panels[level, rows] = result
            copies[level + 1, k] = send(level + 1, k)
            copies[level + 1, k].start()
        else:
            out[rows] = result

    for k in range(len(chunks) + LEVELS - 1):
        for level in range(LEVELS):
            if 0 <= k - level < len(chunks):
                step(level, k - level)
    for copy in copies.values():
        copy.wait_send()


def per_device(n_row, n_col, probes, own_blocks, cross_blocks, level_perm):
    rows, depth = probes.shape
    chunks = row_chunks(rows)
    weights = pltpu.VMEM(own_blocks.shape, jnp.bfloat16)
    return pl.pallas_call(
        functools.partial(kernel, n_row, n_col, chunks),
        out_shape=jax.ShapeDtypeStruct((rows, depth), jnp.bfloat16),
        in_specs=[pl.BlockSpec(memory_space=pltpu.HBM)] * 4,
        out_specs=pl.BlockSpec(memory_space=pltpu.VMEM),
        scratch_shapes=[
            pltpu.VMEM((rows, depth), jnp.bfloat16),
            weights,
            weights,
            pltpu.VMEM(level_perm.shape, jnp.int32),
            weights,
            weights,
            pltpu.VMEM((LEVELS - 1, rows, depth), jnp.bfloat16),
            pltpu.VMEM((LEVELS, rows, depth), jnp.bfloat16),
            pltpu.SemaphoreType.DMA((3,)),
            pltpu.SemaphoreType.DMA,
            pltpu.SemaphoreType.DMA((LEVELS, len(chunks))),
            pltpu.SemaphoreType.DMA((LEVELS, len(chunks))),
        ],
        compiler_params=pltpu.CompilerParams(
            collective_id=0, has_side_effects=True, vmem_limit_bytes=60 * 2**20
        ),
        cost_estimate=pl.CostEstimate(
            flops=24 * rows * depth * depth, bytes_accessed=8 * rows * depth * 2, transcendentals=0
        ),
    )(probes, own_blocks, cross_blocks, level_perm)


def solution(mesh):
    n_row, n_col = mesh.shape["row"], mesh.shape["col"]
    placed = (
        P(None, ("row", "col")),
        P(None, ("row", "col"), None),
        P(None, ("row", "col"), None),
        P(None, ("row", "col")),
    )
    return jax.shard_map(
        functools.partial(per_device, n_row, n_col),
        mesh=mesh,
        in_specs=placed,
        out_specs=P(None, ("row", "col")),
        check_vma=False,
    )
```

```python
import functools

import jax
import jax.numpy as jnp
from jax import lax
from jax.experimental import pallas as pl
from jax.experimental.pallas import tpu as pltpu
from jax.sharding import PartitionSpec as P

LEVELS = 3
BODY = 32
TAIL = (16, 16)
AHEAD = 4
LAG = 96


def row_chunks(rows):
    sizes = list(TAIL) if rows > sum(TAIL) else []
    left = rows - sum(sizes)
    head = [BODY] * (left // BODY)
    if left % BODY:
        head.append(left % BODY)
    chunks, start = [], 0
    for size in head + sizes:
        chunks.append((start, size))
        start += size
    return chunks


def step_order(chunks):
    steps = [(level, k) for k in range(len(chunks)) for level in range(LEVELS)]
    return sorted(steps, key=lambda s: (sum(chunks[s[1]]) + s[0] * LAG, s[0]))


def flip(index, distance):
    return index + distance - 2 * distance * lax.rem(lax.div(index, distance), 2)


def kernel(
    n_row, n_col, chunks,
    probes, own, cross, perm,
    out,
    mine, own_v, cross_v, perm_v, own_p, cross_p, panels, others,
    load_sem, perm_sem, send_sem, recv_sem,
):
    row, col = lax.axis_index("row"), lax.axis_index("col")
    partners = [
        (row, flip(col, n_col // 2)),
        (flip(row, n_row // 2), col),
        (row, flip(col, 1)),
    ]
    barrier = pltpu.get_barrier_semaphore()
    for partner in partners:
        pl.semaphore_signal(
            barrier, inc=1, device_id=partner, device_id_type=pl.DeviceIdType.MESH
        )
    loads = [
        pltpu.make_async_copy(perm, perm_v, perm_sem),
        pltpu.make_async_copy(own, own_v, load_sem.at[0]),
        pltpu.make_async_copy(cross, cross_v, load_sem.at[1]),
        pltpu.make_async_copy(probes, mine, load_sem.at[2]),
    ]
    for load in loads:
        load.start()
    pl.semaphore_wait(barrier, LEVELS)

    def send(level, k):
        start, size = chunks[k]
        rows = pl.ds(start, size)
        source = probes.at[rows] if level == 0 else panels.at[level - 1, rows]
        return pltpu.make_async_remote_copy(
            src_ref=source,
            dst_ref=others.at[level, rows],
            send_sem=send_sem.at[level, k],
            recv_sem=recv_sem.at[level, k],
            device_id=partners[level],
            device_id_type=pl.DeviceIdType.MESH,
        )

    copies = {}
    for k in range(min(AHEAD, len(chunks))):
        copies[0, k] = send(0, k)
        copies[0, k].start()

    for load in loads:
        load.wait()
    depth = own.shape[1]
    for level in range(LEVELS):
        index = lax.broadcasted_iota(jnp.int32, (depth, depth), 0)
        pick = jnp.where(index == perm_v[level : level + 1, :], 1.0, 0.0).astype(jnp.bfloat16)
        for source, target in ((own_v, own_p), (cross_v, cross_p)):
            moved = jnp.dot(source[level], pick, preferred_element_type=jnp.float32)
            target[level] = moved.astype(jnp.bfloat16)

    def step(level, k):
        start, size = chunks[k]
        rows = pl.ds(start, size)
        held = mine[rows] if level == 0 else panels[level - 1, rows]
        total = jnp.dot(held, own_p[level], preferred_element_type=jnp.float32)
        copies[level, k].wait_recv()
        if level == 0 and k + AHEAD < len(chunks):
            copies[0, k + AHEAD] = send(0, k + AHEAD)
            copies[0, k + AHEAD].start()
        total += jnp.dot(others[level, rows], cross_p[level], preferred_element_type=jnp.float32)
        result = total.astype(jnp.bfloat16)
        if level < LEVELS - 1:
            panels[level, rows] = result
            copies[level + 1, k] = send(level + 1, k)
            copies[level + 1, k].start()
        else:
            out[rows] = result

    for level, k in step_order(chunks):
        step(level, k)
    for copy in copies.values():
        copy.wait_send()


def per_device(n_row, n_col, probes, own_blocks, cross_blocks, level_perm):
    rows, depth = probes.shape
    chunks = row_chunks(rows)
    weights = pltpu.VMEM(own_blocks.shape, jnp.bfloat16)
    return pl.pallas_call(
        functools.partial(kernel, n_row, n_col, chunks),
        out_shape=jax.ShapeDtypeStruct((rows, depth), jnp.bfloat16),
        in_specs=[pl.BlockSpec(memory_space=pltpu.HBM)] * 4,
        out_specs=pl.BlockSpec(memory_space=pltpu.VMEM),
        scratch_shapes=[
            pltpu.VMEM((rows, depth), jnp.bfloat16),
            weights,
            weights,
            pltpu.VMEM(level_perm.shape, jnp.int32),
            weights,
            weights,
            pltpu.VMEM((LEVELS - 1, rows, depth), jnp.bfloat16),
            pltpu.VMEM((LEVELS, rows, depth), jnp.bfloat16),
            pltpu.SemaphoreType.DMA((3,)),
            pltpu.SemaphoreType.DMA,
            pltpu.SemaphoreType.DMA((LEVELS, len(chunks))),
            pltpu.SemaphoreType.DMA((LEVELS, len(chunks))),
        ],
        compiler_params=pltpu.CompilerParams(
            collective_id=0, has_side_effects=True, vmem_limit_bytes=60 * 2**20
        ),
        cost_estimate=pl.CostEstimate(
            flops=24 * rows * depth * depth, bytes_accessed=8 * rows * depth * 2, transcendentals=0
        ),
    )(probes, own_blocks, cross_blocks, level_perm)


def solution(mesh):
    n_row, n_col = mesh.shape["row"], mesh.shape["col"]
    placed = (
        P(None, ("row", "col")),
        P(None, ("row", "col"), None),
        P(None, ("row", "col"), None),
        P(None, ("row", "col")),
    )
    return jax.shard_map(
        functools.partial(per_device, n_row, n_col),
        mesh=mesh,
        in_specs=placed,
        out_specs=P(None, ("row", "col")),
        check_vma=False,
    )
```

```python
import functools

import jax
import jax.numpy as jnp
from jax import lax
from jax.experimental import pallas as pl
from jax.experimental.pallas import tpu as pltpu
from jax.sharding import PartitionSpec as P

LEVELS = 3
BODY = 32
TAIL = (16, 16)
AHEAD = 4
LAG = 32


def row_chunks(rows):
    sizes = list(TAIL) if rows > sum(TAIL) else []
    left = rows - sum(sizes)
    head = [BODY] * (left // BODY)
    if left % BODY:
        head.append(left % BODY)
    chunks, start = [], 0
    for size in head + sizes:
        chunks.append((start, size))
        start += size
    return chunks


def step_order(chunks):
    rows = sum(chunks[-1])
    steps = []
    for k, chunk in enumerate(chunks):
        due = sum(chunk)
        for level in range(LEVELS):
            steps.append((due, level, k))
            due += min((AHEAD - 1) * BODY, max(rows - due, 0)) + LAG
    return [(level, k) for _, level, k in sorted(steps)]


def flip(index, distance):
    return index + distance - 2 * distance * lax.rem(lax.div(index, distance), 2)


def kernel(
    n_row, n_col, chunks,
    probes, own, cross, perm,
    out,
    mine, own_v, cross_v, perm_v, own_p, cross_p, panels, others,
    load_sem, perm_sem, send_sem, recv_sem,
):
    row, col = lax.axis_index("row"), lax.axis_index("col")
    partners = [
        (row, flip(col, n_col // 2)),
        (flip(row, n_row // 2), col),
        (row, flip(col, 1)),
    ]
    barrier = pltpu.get_barrier_semaphore()
    for partner in partners:
        pl.semaphore_signal(
            barrier, inc=1, device_id=partner, device_id_type=pl.DeviceIdType.MESH
        )
    loads = [
        pltpu.make_async_copy(perm, perm_v, perm_sem),
        pltpu.make_async_copy(own, own_v, load_sem.at[0]),
        pltpu.make_async_copy(cross, cross_v, load_sem.at[1]),
        pltpu.make_async_copy(probes, mine, load_sem.at[2]),
    ]
    for load in loads:
        load.start()
    pl.semaphore_wait(barrier, LEVELS)

    def send(level, k):
        start, size = chunks[k]
        rows = pl.ds(start, size)
        source = probes.at[rows] if level == 0 else panels.at[level - 1, rows]
        return pltpu.make_async_remote_copy(
            src_ref=source,
            dst_ref=others.at[level, rows],
            send_sem=send_sem.at[level, k],
            recv_sem=recv_sem.at[level, k],
            device_id=partners[level],
            device_id_type=pl.DeviceIdType.MESH,
        )

    copies = {}
    for k in range(min(AHEAD, len(chunks))):
        copies[0, k] = send(0, k)
        copies[0, k].start()

    for load in loads:
        load.wait()
    depth = own.shape[1]
    for level in range(LEVELS):
        index = lax.broadcasted_iota(jnp.int32, (depth, depth), 0)
        pick = jnp.where(index == perm_v[level : level + 1, :], 1.0, 0.0).astype(jnp.bfloat16)
        for source, target in ((own_v, own_p), (cross_v, cross_p)):
            moved = jnp.dot(source[level], pick, preferred_element_type=jnp.float32)
            target[level] = moved.astype(jnp.bfloat16)

    def step(level, k):
        start, size = chunks[k]
        rows = pl.ds(start, size)
        held = mine[rows] if level == 0 else panels[level - 1, rows]
        total = jnp.dot(held, own_p[level], preferred_element_type=jnp.float32)
        copies[level, k].wait_recv()
        total += jnp.dot(others[level, rows], cross_p[level], preferred_element_type=jnp.float32)
        result = total.astype(jnp.bfloat16)
        if level < LEVELS - 1:
            panels[level, rows] = result
            copies[level + 1, k] = send(level + 1, k)
            copies[level + 1, k].start()
        if level == 0 and k + AHEAD < len(chunks):
            copies[0, k + AHEAD] = send(0, k + AHEAD)
            copies[0, k + AHEAD].start()
        else:
            out[rows] = result

    for level, k in step_order(chunks):
        step(level, k)
    for copy in copies.values():
        copy.wait_send()


def per_device(n_row, n_col, probes, own_blocks, cross_blocks, level_perm):
    rows, depth = probes.shape
    chunks = row_chunks(rows)
    weights = pltpu.VMEM(own_blocks.shape, jnp.bfloat16)
    probes, own_blocks, cross_blocks, level_perm = (
        pltpu.with_memory_space_constraint(a, pltpu.HBM)
        for a in (probes, own_blocks, cross_blocks, level_perm)
    )
    return pl.pallas_call(
        functools.partial(kernel, n_row, n_col, chunks),
        out_shape=jax.ShapeDtypeStruct((rows, depth), jnp.bfloat16),
        in_specs=[pl.BlockSpec(memory_space=pltpu.HBM)] * 4,
        out_specs=pl.BlockSpec(memory_space=pltpu.VMEM),
        scratch_shapes=[
            pltpu.VMEM((rows, depth), jnp.bfloat16),
            weights,
            weights,
            pltpu.VMEM(level_perm.shape, jnp.int32),
            weights,
            weights,
            pltpu.VMEM((LEVELS - 1, rows, depth), jnp.bfloat16),
            pltpu.VMEM((LEVELS, rows, depth), jnp.bfloat16),
            pltpu.SemaphoreType.DMA((3,)),
            pltpu.SemaphoreType.DMA,
            pltpu.SemaphoreType.DMA((LEVELS, len(chunks))),
            pltpu.SemaphoreType.DMA((LEVELS, len(chunks))),
        ],
        compiler_params=pltpu.CompilerParams(
            collective_id=0, has_side_effects=True, vmem_limit_bytes=32 * 2**20
        ),
        cost_estimate=pl.CostEstimate(
            flops=24 * rows * depth * depth, bytes_accessed=8 * rows * depth * 2, transcendentals=0
        ),
    )(probes, own_blocks, cross_blocks, level_perm)


def solution(mesh):
    n_row, n_col = mesh.shape["row"], mesh.shape["col"]
    placed = (
        P(None, ("row", "col")),
        P(None, ("row", "col"), None),
        P(None, ("row", "col"), None),
        P(None, ("row", "col")),
    )
    return jax.shard_map(
        functools.partial(per_device, n_row, n_col),
        mesh=mesh,
        in_specs=placed,
        out_specs=P(None, ("row", "col")),
        check_vma=False,
    )
```

```python
import functools

import jax
import jax.numpy as jnp
from jax import lax
from jax.experimental import pallas as pl
from jax.experimental.pallas import tpu as pltpu
from jax.sharding import PartitionSpec as P

LEVELS = 3
BODY = 32
TAIL = (16, 16)
FIRST = 6
AHEAD = 3
LAG = 32


def row_chunks(rows):
    sizes = list(TAIL) if rows > sum(TAIL) else []
    left = rows - sum(sizes)
    head = [BODY] * (left // BODY)
    if left % BODY:
        head.append(left % BODY)
    chunks, start = [], 0
    for size in head + sizes:
        chunks.append((start, size))
        start += size
    return chunks


def step_order(chunks):
    rows = sum(chunks[-1])
    steps = []
    for k, chunk in enumerate(chunks):
        due = sum(chunk)
        for level in range(LEVELS):
            steps.append((due, level, k))
            due += min((AHEAD - 1) * BODY, max(rows - due, 0)) + LAG
    return [(level, k) for _, level, k in sorted(steps)]


def flip(index, distance):
    return index + distance - 2 * distance * lax.rem(lax.div(index, distance), 2)


def kernel(
    n_row, n_col, chunks,
    probes, own, cross, perm,
    out,
    mine, own_v, cross_v, perm_v, own_p, cross_p, panels, others,
    load_sem, perm_sem, send_sem, recv_sem,
):
    row, col = lax.axis_index("row"), lax.axis_index("col")
    partners = [
        (row, flip(col, n_col // 2)),
        (flip(row, n_row // 2), col),
        (row, flip(col, 1)),
    ]
    barrier = pltpu.get_barrier_semaphore()
    for partner in partners:
        pl.semaphore_signal(
            barrier, inc=1, device_id=partner, device_id_type=pl.DeviceIdType.MESH
        )
    loads = [
        pltpu.make_async_copy(perm, perm_v, perm_sem),
        pltpu.make_async_copy(own, own_v, load_sem.at[0]),
        pltpu.make_async_copy(cross, cross_v, load_sem.at[1]),
        pltpu.make_async_copy(probes, mine, load_sem.at[2]),
    ]
    for load in loads:
        load.start()
    pl.semaphore_wait(barrier, LEVELS)

    def send(level, k):
        start, size = chunks[k]
        rows = pl.ds(start, size)
        source = probes.at[rows] if level == 0 else panels.at[level - 1, rows]
        return pltpu.make_async_remote_copy(
            src_ref=source,
            dst_ref=others.at[level, rows],
            send_sem=send_sem.at[level, k],
            recv_sem=recv_sem.at[level, k],
            device_id=partners[level],
            device_id_type=pl.DeviceIdType.MESH,
        )

    copies = {}
    for k in range(min(FIRST, len(chunks))):
        copies[0, k] = send(0, k)
        copies[0, k].start()

    for load in loads:
        load.wait()
    depth = own.shape[1]
    for level in range(LEVELS):
        index = lax.broadcasted_iota(jnp.int32, (depth, depth), 0)
        pick = jnp.where(index == perm_v[level : level + 1, :], 1.0, 0.0).astype(jnp.bfloat16)
        for source, target in ((own_v, own_p), (cross_v, cross_p)):
            moved = jnp.dot(source[level], pick, preferred_element_type=jnp.float32)
            target[level] = moved.astype(jnp.bfloat16)

    def step(level, k):
        start, size = chunks[k]
        rows = pl.ds(start, size)
        held = mine[rows] if level == 0 else panels[level - 1, rows]
        total = jnp.dot(held, own_p[level], preferred_element_type=jnp.float32)
        copies[level, k].wait_recv()
        total += jnp.dot(others[level, rows], cross_p[level], preferred_element_type=jnp.float32)
        result = total.astype(jnp.bfloat16)
        if level < LEVELS - 1:
            panels[level, rows] = result
            copies[level + 1, k] = send(level + 1, k)
            copies[level + 1, k].start()
        else:
            out[rows] = result
        if level == 0 and FIRST <= k + AHEAD < len(chunks):
            copies[0, k].wait_send()
            copies[0, k + AHEAD] = send(0, k + AHEAD)
            copies[0, k + AHEAD].start()

    for level, k in step_order(chunks):
        step(level, k)
    for (level, k), copy in copies.items():
        if level > 0 or not FIRST <= k + AHEAD < len(chunks):
            copy.wait_send()


def per_device(n_row, n_col, probes, own_blocks, cross_blocks, level_perm):
    rows, depth = probes.shape
    chunks = row_chunks(rows)
    weights = pltpu.VMEM(own_blocks.shape, jnp.bfloat16)
    probes, own_blocks, cross_blocks, level_perm = (
        pltpu.with_memory_space_constraint(a, pltpu.HBM)
        for a in (probes, own_blocks, cross_blocks, level_perm)
    )
    return pl.pallas_call(
        functools.partial(kernel, n_row, n_col, chunks),
        out_shape=jax.ShapeDtypeStruct((rows, depth), jnp.bfloat16),
        in_specs=[pl.BlockSpec(memory_space=pltpu.HBM)] * 4,
        out_specs=pl.BlockSpec(memory_space=pltpu.VMEM),
        scratch_shapes=[
            pltpu.VMEM((rows, depth), jnp.bfloat16),
            weights,
            weights,
            pltpu.VMEM(level_perm.shape, jnp.int32),
            weights,
            weights,
            pltpu.VMEM((LEVELS - 1, rows, depth), jnp.bfloat16),
            pltpu.VMEM((LEVELS, rows, depth), jnp.bfloat16),
            pltpu.SemaphoreType.DMA((3,)),
            pltpu.SemaphoreType.DMA,
            pltpu.SemaphoreType.DMA((LEVELS, len(chunks))),
            pltpu.SemaphoreType.DMA((LEVELS, len(chunks))),
        ],
        compiler_params=pltpu.CompilerParams(
            collective_id=0, has_side_effects=True, vmem_limit_bytes=32 * 2**20
        ),
        cost_estimate=pl.CostEstimate(
            flops=24 * rows * depth * depth, bytes_accessed=8 * rows * depth * 2, transcendentals=0
        ),
    )(probes, own_blocks, cross_blocks, level_perm)


def solution(mesh):
    n_row, n_col = mesh.shape["row"], mesh.shape["col"]
    placed = (
        P(None, ("row", "col")),
        P(None, ("row", "col"), None),
        P(None, ("row", "col"), None),
        P(None, ("row", "col")),
    )
    return jax.shard_map(
        functools.partial(per_device, n_row, n_col),
        mesh=mesh,
        in_specs=placed,
        out_specs=P(None, ("row", "col")),
        check_vma=False,
    )
```

```python
import functools

import jax
import jax.numpy as jnp
from jax import lax
from jax.experimental import pallas as pl
from jax.experimental.pallas import tpu as pltpu
from jax.sharding import PartitionSpec as P

LEVELS = 3
BODY = 64
TAIL = (32, 32, 32, 16, 16)
AHEAD = 3
NEAR = 40
FAR = 160
JOIN = 128


def row_chunks(rows):
    sizes = list(TAIL) if rows > sum(TAIL) else []
    left = rows - sum(sizes)
    head = [BODY] * (left // BODY)
    if left % BODY:
        head.append(left % BODY)
    chunks, start = [], 0
    for size in head + sizes:
        chunks.append((start, size))
        start += size
    return chunks


def step_order(chunks):
    rows = sum(chunks[-1])
    steps, group = [], []
    for k, chunk in enumerate(chunks):
        due = sum(chunk)
        for level in range(LEVELS - 1):
            steps.append((due, level, (k,)))
            due += max(NEAR, min(FAR, 3 * (rows - due) // 4))
        group.append(k)
        size = sum(chunks[j][1] for j in group)
        if size >= JOIN or k >= len(chunks) - 3 or k == len(chunks) - 1:
            steps.append((due, LEVELS - 1, tuple(group)))
            group = []
    return [(level, ks) for _, level, ks in sorted(steps)]


def flip(index, distance):
    return index + distance - 2 * distance * lax.rem(lax.div(index, distance), 2)


def kernel(
    n_row, n_col, chunks,
    probes, own, cross, perm,
    out,
    mine, own_v, cross_v, perm_v, own_p, cross_p, panels, others,
    load_sem, perm_sem, send_sem, recv_sem,
):
    row, col = lax.axis_index("row"), lax.axis_index("col")
    partners = [
        (row, flip(col, n_col // 2)),
        (flip(row, n_row // 2), col),
        (row, flip(col, 1)),
    ]
    barrier = pltpu.get_barrier_semaphore()
    for partner in partners:
        pl.semaphore_signal(
            barrier, inc=1, device_id=partner, device_id_type=pl.DeviceIdType.MESH
        )
    loads = [
        pltpu.make_async_copy(perm, perm_v, perm_sem),
        pltpu.make_async_copy(own, own_v, load_sem.at[0]),
        pltpu.make_async_copy(cross, cross_v, load_sem.at[1]),
        pltpu.make_async_copy(probes, mine, load_sem.at[2]),
    ]
    for load in loads:
        load.start()
    pl.semaphore_wait(barrier, LEVELS)

    def send(level, k):
        start, size = chunks[k]
        rows = pl.ds(start, size)
        source = probes.at[rows] if level == 0 else panels.at[level - 1, rows]
        return pltpu.make_async_remote_copy(
            src_ref=source,
            dst_ref=others.at[level, rows],
            send_sem=send_sem.at[level, k],
            recv_sem=recv_sem.at[level, k],
            device_id=partners[level],
            device_id_type=pl.DeviceIdType.MESH,
        )

    copies = {}
    for k in range(min(AHEAD, len(chunks))):
        copies[0, k] = send(0, k)
        copies[0, k].start()

    for load in loads:
        load.wait()
    depth = own.shape[1]
    for level in range(LEVELS):
        index = lax.broadcasted_iota(jnp.int32, (depth, depth), 0)
        pick = jnp.where(index == perm_v[level : level + 1, :], 1.0, 0.0).astype(jnp.bfloat16)
        for source, target in ((own_v, own_p), (cross_v, cross_p)):
            moved = jnp.dot(source[level], pick, preferred_element_type=jnp.float32)
            target[level] = moved.astype(jnp.bfloat16)

    def step(level, ks):
        start, k = chunks[ks[0]][0], ks[-1]
        rows = pl.ds(start, sum(chunks[k]) - start)
        held = mine[rows] if level == 0 else panels[level - 1, rows]
        total = jnp.dot(held, own_p[level], preferred_element_type=jnp.float32)
        for j in ks:
            copies[level, j].wait_recv()
        total += jnp.dot(others[level, rows], cross_p[level], preferred_element_type=jnp.float32)
        result = total.astype(jnp.bfloat16)
        if level == LEVELS - 1:
            out[rows] = result
            return
        panels[level, rows] = result
        copies[level + 1, k] = send(level + 1, k)
        copies[level + 1, k].start()
        if level == 0 and k + AHEAD < len(chunks):
            copies[0, k + AHEAD] = send(0, k + AHEAD)
            copies[0, k + AHEAD].start()

    for level, ks in step_order(chunks):
        step(level, ks)
    for copy in copies.values():
        copy.wait_send()


def per_device(n_row, n_col, probes, own_blocks, cross_blocks, level_perm):
    rows, depth = probes.shape
    chunks = row_chunks(rows)
    weights = pltpu.VMEM(own_blocks.shape, jnp.bfloat16)
    probes, own_blocks, cross_blocks, level_perm = (
        pltpu.with_memory_space_constraint(a, pltpu.HBM)
        for a in (probes, own_blocks, cross_blocks, level_perm)
    )
    return pl.pallas_call(
        functools.partial(kernel, n_row, n_col, chunks),
        out_shape=jax.ShapeDtypeStruct((rows, depth), jnp.bfloat16),
        in_specs=[pl.BlockSpec(memory_space=pltpu.HBM)] * 4,
        out_specs=pl.BlockSpec(memory_space=pltpu.VMEM),
        scratch_shapes=[
            pltpu.VMEM((rows, depth), jnp.bfloat16),
            weights,
            weights,
            pltpu.VMEM(level_perm.shape, jnp.int32),
            weights,
            weights,
            pltpu.VMEM((LEVELS - 1, rows, depth), jnp.bfloat16),
            pltpu.VMEM((LEVELS, rows, depth), jnp.bfloat16),
            pltpu.SemaphoreType.DMA((3,)),
            pltpu.SemaphoreType.DMA,
            pltpu.SemaphoreType.DMA((LEVELS, len(chunks))),
            pltpu.SemaphoreType.DMA((LEVELS, len(chunks))),
        ],
        compiler_params=pltpu.CompilerParams(
            collective_id=0, has_side_effects=True, vmem_limit_bytes=32 * 2**20
        ),
        cost_estimate=pl.CostEstimate(
            flops=24 * rows * depth * depth, bytes_accessed=8 * rows * depth * 2, transcendentals=0
        ),
    )(probes, own_blocks, cross_blocks, level_perm)


def solution(mesh):
    n_row, n_col = mesh.shape["row"], mesh.shape["col"]
    placed = (
        P(None, ("row", "col")),
        P(None, ("row", "col"), None),
        P(None, ("row", "col"), None),
        P(None, ("row", "col")),
    )
    return jax.shard_map(
        functools.partial(per_device, n_row, n_col),
        mesh=mesh,
        in_specs=placed,
        out_specs=P(None, ("row", "col")),
        check_vma=False,
    )
```

```python
import functools

import jax
import jax.numpy as jnp
from jax import lax
from jax.experimental import pallas as pl
from jax.experimental.pallas import tpu as pltpu
from jax.sharding import PartitionSpec as P

LEVELS = 3
BODY = 64
TAIL = (32, 32, 32, 16, 16)
NEAR = 64
FAR = 160
JOIN = 128


def row_chunks(rows):
    sizes = list(TAIL) if rows > sum(TAIL) else []
    left = rows - sum(sizes)
    head = [BODY] * (left // BODY)
    if left % BODY:
        head.append(left % BODY)
    chunks, start = [], 0
    for size in head + sizes:
        chunks.append((start, size))
        start += size
    return chunks


def step_order(chunks):
    rows = sum(chunks[-1])
    steps, group = [], []
    for k, chunk in enumerate(chunks):
        due = sum(chunk)
        for level in range(LEVELS - 1):
            steps.append((due, level, (k,)))
            due += max(NEAR, min(FAR, 3 * (rows - due) // 4))
        group.append(k)
        size = sum(chunks[j][1] for j in group)
        if size >= JOIN or k >= len(chunks) - 3 or k == len(chunks) - 1:
            steps.append((due, LEVELS - 1, tuple(group)))
            group = []
    return [(level, ks) for _, level, ks in sorted(steps)]


def flip(index, distance):
    return index + distance - 2 * distance * lax.rem(lax.div(index, distance), 2)


def kernel(
    n_row, n_col, chunks,
    probes, own, cross, perm,
    out,
    mine, own_v, cross_v, perm_v, own_p, cross_p, panels, others,
    load_sem, perm_sem, send_sem, recv_sem,
):
    row, col = lax.axis_index("row"), lax.axis_index("col")
    partners = [
        (row, flip(col, n_col // 2)),
        (flip(row, n_row // 2), col),
        (row, flip(col, 1)),
    ]
    barrier = pltpu.get_barrier_semaphore()
    for partner in partners:
        pl.semaphore_signal(
            barrier, inc=1, device_id=partner, device_id_type=pl.DeviceIdType.MESH
        )
    loads = [
        pltpu.make_async_copy(perm, perm_v, perm_sem),
        pltpu.make_async_copy(own, own_v, load_sem.at[0]),
        pltpu.make_async_copy(cross, cross_v, load_sem.at[1]),
        pltpu.make_async_copy(probes, mine, load_sem.at[2]),
    ]
    for load in loads:
        load.start()
    pl.semaphore_wait(barrier, LEVELS)

    def send(level, k):
        start, size = chunks[k]
        rows = pl.ds(start, size)
        source = probes.at[rows] if level == 0 else panels.at[level - 1, rows]
        return pltpu.make_async_remote_copy(
            src_ref=source,
            dst_ref=others.at[level, rows],
            send_sem=send_sem.at[level, k],
            recv_sem=recv_sem.at[level, k],
            device_id=partners[level],
            device_id_type=pl.DeviceIdType.MESH,
        )

    copies = {}
    for k in range(len(chunks)):
        copies[0, k] = send(0, k)
        copies[0, k].start()

    for load in loads:
        load.wait()
    depth = own.shape[1]
    for level in range(LEVELS):
        index = lax.broadcasted_iota(jnp.int32, (depth, depth), 0)
        pick = jnp.where(index == perm_v[level : level + 1, :], 1.0, 0.0).astype(jnp.bfloat16)
        for source, target in ((own_v, own_p), (cross_v, cross_p)):
            moved = jnp.dot(source[level], pick, preferred_element_type=jnp.float32)
            target[level] = moved.astype(jnp.bfloat16)

    def step(level, ks):
        start, k = chunks[ks[0]][0], ks[-1]
        rows = pl.ds(start, sum(chunks[k]) - start)
        held = mine[rows] if level == 0 else panels[level - 1, rows]
        total = jnp.dot(held, own_p[level], preferred_element_type=jnp.float32)
        for j in ks:
            copies[level, j].wait_recv()
        total += jnp.dot(others[level, rows], cross_p[level], preferred_element_type=jnp.float32)
        result = total.astype(jnp.bfloat16)
        if level == LEVELS - 1:
            out[rows] = result
            return
        panels[level, rows] = result
        copies[level + 1, k] = send(level + 1, k)
        copies[level + 1, k].start()

    for level, ks in step_order(chunks):
        step(level, ks)
    for copy in copies.values():
        copy.wait_send()


def per_device(n_row, n_col, probes, own_blocks, cross_blocks, level_perm):
    rows, depth = probes.shape
    chunks = row_chunks(rows)
    weights = pltpu.VMEM(own_blocks.shape, jnp.bfloat16)
    probes, own_blocks, cross_blocks, level_perm = (
        pltpu.with_memory_space_constraint(a, pltpu.HBM)
        for a in (probes, own_blocks, cross_blocks, level_perm)
    )
    return pl.pallas_call(
        functools.partial(kernel, n_row, n_col, chunks),
        out_shape=jax.ShapeDtypeStruct((rows, depth), jnp.bfloat16),
        in_specs=[pl.BlockSpec(memory_space=pltpu.HBM)] * 4,
        out_specs=pl.BlockSpec(memory_space=pltpu.VMEM),
        scratch_shapes=[
            pltpu.VMEM((rows, depth), jnp.bfloat16),
            weights,
            weights,
            pltpu.VMEM(level_perm.shape, jnp.int32),
            weights,
            weights,
            pltpu.VMEM((LEVELS - 1, rows, depth), jnp.bfloat16),
            pltpu.VMEM((LEVELS, rows, depth), jnp.bfloat16),
            pltpu.SemaphoreType.DMA((3,)),
            pltpu.SemaphoreType.DMA,
            pltpu.SemaphoreType.DMA((LEVELS, len(chunks))),
            pltpu.SemaphoreType.DMA((LEVELS, len(chunks))),
        ],
        compiler_params=pltpu.CompilerParams(
            collective_id=0, has_side_effects=True, vmem_limit_bytes=32 * 2**20
        ),
        cost_estimate=pl.CostEstimate(
            flops=24 * rows * depth * depth, bytes_accessed=8 * rows * depth * 2, transcendentals=0
        ),
    )(probes, own_blocks, cross_blocks, level_perm)


def solution(mesh):
    n_row, n_col = mesh.shape["row"], mesh.shape["col"]
    placed = (
        P(None, ("row", "col")),
        P(None, ("row", "col"), None),
        P(None, ("row", "col"), None),
        P(None, ("row", "col")),
    )
    return jax.shard_map(
        functools.partial(per_device, n_row, n_col),
        mesh=mesh,
        in_specs=placed,
        out_specs=P(None, ("row", "col")),
        check_vma=False,
    )
```

```python
import functools

import jax
import jax.numpy as jnp
from jax import lax
from jax.experimental import pallas as pl
from jax.experimental.pallas import tpu as pltpu
from jax.sharding import PartitionSpec as P

LEVELS = 3
BODY = 64
TAIL = (32, 32, 32, 16, 16)
AHEAD = 2
NEAR = 64
FAR = 112
JOIN = 128


def row_chunks(rows):
    sizes = list(TAIL) if rows > sum(TAIL) else []
    left = rows - sum(sizes)
    head = [BODY] * (left // BODY)
    if left % BODY:
        head.append(left % BODY)
    chunks, start = [], 0
    for size in head + sizes:
        chunks.append((start, size))
        start += size
    return chunks


def step_order(chunks):
    rows = sum(chunks[-1])
    steps, group = [], []
    for k, chunk in enumerate(chunks):
        due = sum(chunk)
        for level in range(LEVELS - 1):
            steps.append((due, level, (k,)))
            due += max(NEAR, min(FAR, 3 * (rows - due) // 4))
        group.append(k)
        size = sum(chunks[j][1] for j in group)
        if size >= JOIN or k >= len(chunks) - 3 or k == len(chunks) - 1:
            steps.append((due, LEVELS - 1, tuple(group)))
            group = []
    return [(level, ks) for _, level, ks in sorted(steps)]


def flip(index, distance):
    return index + distance - 2 * distance * lax.rem(lax.div(index, distance), 2)


def kernel(
    n_row, n_col, chunks,
    probes, own, cross, perm,
    out,
    mine, own_v, cross_v, perm_v, own_p, cross_p, panels, others,
    load_sem, perm_sem, send_sem, recv_sem,
):
    row, col = lax.axis_index("row"), lax.axis_index("col")
    partners = [
        (row, flip(col, n_col // 2)),
        (flip(row, n_row // 2), col),
        (row, flip(col, 1)),
    ]
    barrier = pltpu.get_barrier_semaphore()
    for partner in partners:
        pl.semaphore_signal(
            barrier, inc=1, device_id=partner, device_id_type=pl.DeviceIdType.MESH
        )
    loads = [
        pltpu.make_async_copy(perm, perm_v, perm_sem),
        pltpu.make_async_copy(own, own_v, load_sem.at[0]),
        pltpu.make_async_copy(cross, cross_v, load_sem.at[1]),
        pltpu.make_async_copy(probes, mine, load_sem.at[2]),
    ]
    for load in loads:
        load.start()
    pl.semaphore_wait(barrier, LEVELS)

    def send(level, k):
        start, size = chunks[k]
        rows = pl.ds(start, size)
        source = probes.at[rows] if level == 0 else panels.at[level - 1, rows]
        return pltpu.make_async_remote_copy(
            src_ref=source,
            dst_ref=others.at[level, rows],
            send_sem=send_sem.at[level, k],
            recv_sem=recv_sem.at[level, k],
            device_id=partners[level],
            device_id_type=pl.DeviceIdType.MESH,
        )

    copies = {}
    for k in range(len(chunks)):
        copies[0, k] = send(0, k)
        if k < AHEAD:
            copies[0, k].start()

    slab = lax.div(col, 2)
    beside = (slab == n_col // 4 - 1) | (slab == n_col // 4)

    @pl.when(beside)
    def _():
        for k in range(AHEAD, len(chunks)):
            copies[0, k].start()

    for load in loads:
        load.wait()
    depth = own.shape[1]
    for level in range(LEVELS):
        index = lax.broadcasted_iota(jnp.int32, (depth, depth), 0)
        pick = jnp.where(index == perm_v[level : level + 1, :], 1.0, 0.0).astype(jnp.bfloat16)
        for source, target in ((own_v, own_p), (cross_v, cross_p)):
            moved = jnp.dot(source[level], pick, preferred_element_type=jnp.float32)
            target[level] = moved.astype(jnp.bfloat16)

    def step(level, ks):
        start, k = chunks[ks[0]][0], ks[-1]
        rows = pl.ds(start, sum(chunks[k]) - start)
        held = mine[rows] if level == 0 else panels[level - 1, rows]
        total = jnp.dot(held, own_p[level], preferred_element_type=jnp.float32)
        for j in ks:
            copies[level, j].wait_recv()
        total += jnp.dot(others[level, rows], cross_p[level], preferred_element_type=jnp.float32)
        result = total.astype(jnp.bfloat16)
        if level == LEVELS - 1:
            out[rows] = result
            return
        panels[level, rows] = result
        copies[level + 1, k] = send(level + 1, k)
        copies[level + 1, k].start()
        if level == 0 and k + AHEAD < len(chunks):
            pl.when(jnp.logical_not(beside))(copies[0, k + AHEAD].start)

    for level, ks in step_order(chunks):
        step(level, ks)
    for copy in copies.values():
        copy.wait_send()


def per_device(n_row, n_col, probes, own_blocks, cross_blocks, level_perm):
    rows, depth = probes.shape
    chunks = row_chunks(rows)
    weights = pltpu.VMEM(own_blocks.shape, jnp.bfloat16)
    probes, own_blocks, cross_blocks, level_perm = (
        pltpu.with_memory_space_constraint(a, pltpu.HBM)
        for a in (probes, own_blocks, cross_blocks, level_perm)
    )
    return pl.pallas_call(
        functools.partial(kernel, n_row, n_col, chunks),
        out_shape=jax.ShapeDtypeStruct((rows, depth), jnp.bfloat16),
        in_specs=[pl.BlockSpec(memory_space=pltpu.HBM)] * 4,
        out_specs=pl.BlockSpec(memory_space=pltpu.VMEM),
        scratch_shapes=[
            pltpu.VMEM((rows, depth), jnp.bfloat16),
            weights,
            weights,
            pltpu.VMEM(level_perm.shape, jnp.int32),
            weights,
            weights,
            pltpu.VMEM((LEVELS - 1, rows, depth), jnp.bfloat16),
            pltpu.VMEM((LEVELS, rows, depth), jnp.bfloat16),
            pltpu.SemaphoreType.DMA((3,)),
            pltpu.SemaphoreType.DMA,
            pltpu.SemaphoreType.DMA((LEVELS, len(chunks))),
            pltpu.SemaphoreType.DMA((LEVELS, len(chunks))),
        ],
        compiler_params=pltpu.CompilerParams(
            collective_id=0, has_side_effects=True, vmem_limit_bytes=32 * 2**20
        ),
        cost_estimate=pl.CostEstimate(
            flops=24 * rows * depth * depth, bytes_accessed=8 * rows * depth * 2, transcendentals=0
        ),
    )(probes, own_blocks, cross_blocks, level_perm)


def solution(mesh):
    n_row, n_col = mesh.shape["row"], mesh.shape["col"]
    placed = (
        P(None, ("row", "col")),
        P(None, ("row", "col"), None),
        P(None, ("row", "col"), None),
        P(None, ("row", "col")),
    )
    return jax.shard_map(
        functools.partial(per_device, n_row, n_col),
        mesh=mesh,
        in_specs=placed,
        out_specs=P(None, ("row", "col")),
        check_vma=False,
    )
```

```python
import functools

import jax
import jax.numpy as jnp
from jax import lax
from jax.experimental import pallas as pl
from jax.experimental.pallas import tpu as pltpu
from jax.sharding import PartitionSpec as P

LEVELS = 3
BODY = 128
TAIL = (96, 64, 48, 32, 16)
AHEAD = 3
LAG = 56


def row_chunks(rows):
    sizes = list(TAIL) if rows > sum(TAIL) else []
    left = rows - sum(sizes)
    head = [BODY] * (left // BODY)
    if left % BODY:
        head.append(left % BODY)
    chunks, start = [], 0
    for size in head + sizes:
        chunks.append((start, size))
        start += size
    return chunks


def step_order(chunks):
    steps = []
    for k, (start, size) in enumerate(chunks):
        for level in range(LEVELS):
            steps.append((start + size + level * (LAG + size // 2), level, k))
    return [(level, k) for _, level, k in sorted(steps)]


def flip(index, distance):
    return index + distance - 2 * distance * lax.rem(lax.div(index, distance), 2)


def kernel(
    n_row, n_col, chunks,
    probes, own, cross, perm,
    out,
    mine, own_v, cross_v, perm_v, own_p, cross_p, panels, others, base,
    load_sem, perm_sem, send_sem, recv_sem,
):
    row, col = lax.axis_index("row"), lax.axis_index("col")
    partners = [
        (row, flip(col, n_col // 2)),
        (flip(row, n_row // 2), col),
        (row, flip(col, 1)),
    ]
    barrier = pltpu.get_barrier_semaphore()
    for partner in partners:
        pl.semaphore_signal(
            barrier, inc=1, device_id=partner, device_id_type=pl.DeviceIdType.MESH
        )
    loads = [
        pltpu.make_async_copy(perm, perm_v, perm_sem),
        pltpu.make_async_copy(own, own_v, load_sem.at[0]),
        pltpu.make_async_copy(cross, cross_v, load_sem.at[1]),
        pltpu.make_async_copy(probes, mine, load_sem.at[2]),
    ]
    for load in loads:
        load.start()
    pl.semaphore_wait(barrier, LEVELS)

    def send(level, k):
        start, size = chunks[k]
        rows = pl.ds(start, size)
        source = probes.at[rows] if level == 0 else panels.at[level - 1, rows]
        return pltpu.make_async_remote_copy(
            src_ref=source,
            dst_ref=others.at[level, rows],
            send_sem=send_sem.at[level, k],
            recv_sem=recv_sem.at[level, k],
            device_id=partners[level],
            device_id_type=pl.DeviceIdType.MESH,
        )

    copies = {}
    for k in range(len(chunks)):
        copies[0, k] = send(0, k)
        if k < AHEAD:
            copies[0, k].start()

    slab = lax.div(col, 2)
    beside = (slab == n_col // 4 - 1) | (slab == n_col // 4)

    @pl.when(beside)
    def _():
        for k in range(AHEAD, len(chunks)):
            copies[0, k].start()

    for load in loads:
        load.wait()
    depth = own.shape[1]
    for level in range(LEVELS):
        index = lax.broadcasted_iota(jnp.int32, (depth, depth), 0)
        pick = jnp.where(index == perm_v[level : level + 1, :], 1.0, 0.0).astype(jnp.bfloat16)
        for source, target in ((own_v, own_p), (cross_v, cross_p)):
            moved = jnp.dot(source[level], pick, preferred_element_type=jnp.float32)
            target[level] = moved.astype(jnp.bfloat16)

    base[...] = jnp.dot(mine[...], own_p[0], preferred_element_type=jnp.float32)

    def step(level, k):
        rows = pl.ds(*chunks[k])
        if level == 0:
            total = base[rows]
        else:
            total = jnp.dot(panels[level - 1, rows], own_p[level], preferred_element_type=jnp.float32)
        copies[level, k].wait_recv()
        total += jnp.dot(others[level, rows], cross_p[level], preferred_element_type=jnp.float32)
        result = total.astype(jnp.bfloat16)
        if level == LEVELS - 1:
            out[rows] = result
            return
        panels[level, rows] = result
        copies[level + 1, k] = send(level + 1, k)
        copies[level + 1, k].start()
        if level == 0 and k + AHEAD < len(chunks):
            pl.when(jnp.logical_not(beside))(copies[0, k + AHEAD].start)

    for level, k in step_order(chunks):
        step(level, k)
    for copy in copies.values():
        copy.wait_send()


def per_device(n_row, n_col, probes, own_blocks, cross_blocks, level_perm):
    rows, depth = probes.shape
    chunks = row_chunks(rows)
    weights = pltpu.VMEM(own_blocks.shape, jnp.bfloat16)
    probes, own_blocks, cross_blocks, level_perm = (
        pltpu.with_memory_space_constraint(a, pltpu.HBM)
        for a in (probes, own_blocks, cross_blocks, level_perm)
    )
    return pl.pallas_call(
        functools.partial(kernel, n_row, n_col, chunks),
        out_shape=jax.ShapeDtypeStruct((rows, depth), jnp.bfloat16),
        in_specs=[pl.BlockSpec(memory_space=pltpu.HBM)] * 4,
        out_specs=pl.BlockSpec(memory_space=pltpu.VMEM),
        scratch_shapes=[
            pltpu.VMEM((rows, depth), jnp.bfloat16),
            weights,
            weights,
            pltpu.VMEM(level_perm.shape, jnp.int32),
            weights,
            weights,
            pltpu.VMEM((LEVELS - 1, rows, depth), jnp.bfloat16),
            pltpu.VMEM((LEVELS, rows, depth), jnp.bfloat16),
            pltpu.VMEM((rows, depth), jnp.float32),
            pltpu.SemaphoreType.DMA((3,)),
            pltpu.SemaphoreType.DMA,
            pltpu.SemaphoreType.DMA((LEVELS, len(chunks))),
            pltpu.SemaphoreType.DMA((LEVELS, len(chunks))),
        ],
        compiler_params=pltpu.CompilerParams(
            collective_id=0, has_side_effects=True, vmem_limit_bytes=32 * 2**20
        ),
        cost_estimate=pl.CostEstimate(
            flops=24 * rows * depth * depth, bytes_accessed=8 * rows * depth * 2, transcendentals=0
        ),
    )(probes, own_blocks, cross_blocks, level_perm)


def solution(mesh):
    n_row, n_col = mesh.shape["row"], mesh.shape["col"]
    placed = (
        P(None, ("row", "col")),
        P(None, ("row", "col"), None),
        P(None, ("row", "col"), None),
        P(None, ("row", "col")),
    )
    return jax.shard_map(
        functools.partial(per_device, n_row, n_col),
        mesh=mesh,
        in_specs=placed,
        out_specs=P(None, ("row", "col")),
        check_vma=False,
    )
```

```python
import functools

import jax
import jax.numpy as jnp
from jax import lax
from jax.experimental import pallas as pl
from jax.experimental.pallas import tpu as pltpu
from jax.sharding import PartitionSpec as P

LEVELS = 3
BODY = 64
TAIL = (48, 32, 32, 16)
AHEAD = 3
NEAR = 48
FAR = 112
JOIN = 128


def row_chunks(rows):
    sizes = list(TAIL) if rows > sum(TAIL) else []
    left = rows - sum(sizes)
    head = [BODY] * (left // BODY)
    if left % BODY:
        head.append(left % BODY)
    chunks, start = [], 0
    for size in head + sizes:
        chunks.append((start, size))
        start += size
    return chunks


def step_order(chunks):
    rows = sum(chunks[-1])
    steps, group = [], []
    for k, chunk in enumerate(chunks):
        due = sum(chunk)
        for level in range(LEVELS - 1):
            steps.append((due, level, (k,)))
            due += max(NEAR, min(FAR, 3 * (rows - due) // 4))
        group.append(k)
        if sum(chunks[j][1] for j in group) >= JOIN or len(chunks) - k in (1, 3):
            steps.append((due, LEVELS - 1, tuple(group)))
            group = []
    return [(level, ks) for _, level, ks in sorted(steps)]


def flip(index, distance):
    return index + distance - 2 * distance * lax.rem(lax.div(index, distance), 2)


def kernel(
    n_row, n_col, chunks,
    probes, own, cross, perm,
    out,
    mine, own_v, cross_v, perm_v, own_p, cross_p, panels, others, base,
    load_sem, perm_sem, send_sem, recv_sem,
):
    row, col = lax.axis_index("row"), lax.axis_index("col")
    partners = [
        (row, flip(col, n_col // 2)),
        (flip(row, n_row // 2), col),
        (row, flip(col, 1)),
    ]
    barrier = pltpu.get_barrier_semaphore()
    for partner in partners:
        pl.semaphore_signal(
            barrier, inc=1, device_id=partner, device_id_type=pl.DeviceIdType.MESH
        )
    loads = [
        pltpu.make_async_copy(perm, perm_v, perm_sem),
        pltpu.make_async_copy(own, own_v, load_sem.at[0]),
        pltpu.make_async_copy(cross, cross_v, load_sem.at[1]),
        pltpu.make_async_copy(probes, mine, load_sem.at[2]),
    ]
    for load in loads:
        load.start()
    pl.semaphore_wait(barrier, LEVELS)

    def send(level, k):
        start, size = chunks[k]
        rows = pl.ds(start, size)
        source = probes.at[rows] if level == 0 else panels.at[level - 1, rows]
        return pltpu.make_async_remote_copy(
            src_ref=source,
            dst_ref=others.at[level, rows],
            send_sem=send_sem.at[level, k],
            recv_sem=recv_sem.at[level, k],
            device_id=partners[level],
            device_id_type=pl.DeviceIdType.MESH,
        )

    copies = {}
    for k in range(min(AHEAD, len(chunks))):
        copies[0, k] = send(0, k)
        copies[0, k].start()

    for load in loads:
        load.wait()
    depth = own.shape[1]
    for level in range(LEVELS):
        index = lax.broadcasted_iota(jnp.int32, (depth, depth), 0)
        pick = jnp.where(index == perm_v[level : level + 1, :], 1.0, 0.0).astype(jnp.bfloat16)
        for source, target in ((own_v, own_p), (cross_v, cross_p)):
            moved = jnp.dot(source[level], pick, preferred_element_type=jnp.float32)
            target[level] = moved.astype(jnp.bfloat16)

    base[...] = jnp.dot(mine[...], own_p[0], preferred_element_type=jnp.float32)

    def step(level, ks):
        start, k = chunks[ks[0]][0], ks[-1]
        rows = pl.ds(start, sum(chunks[k]) - start)
        if level == 0:
            total = base[rows]
        else:
            total = jnp.dot(panels[level - 1, rows], own_p[level], preferred_element_type=jnp.float32)
        for j in ks:
            copies[level, j].wait_recv()
        total += jnp.dot(others[level, rows], cross_p[level], preferred_element_type=jnp.float32)
        result = total.astype(jnp.bfloat16)
        if level == LEVELS - 1:
            out[rows] = result
            return
        panels[level, rows] = result
        copies[level + 1, k] = send(level + 1, k)
        copies[level + 1, k].start()
        if level == 0 and k + AHEAD < len(chunks):
            copies[0, k + AHEAD] = send(0, k + AHEAD)
            copies[0, k + AHEAD].start()

    for level, ks in step_order(chunks):
        step(level, ks)
    for copy in copies.values():
        copy.wait_send()


def per_device(n_row, n_col, probes, own_blocks, cross_blocks, level_perm):
    rows, depth = probes.shape
    chunks = row_chunks(rows)
    weights = pltpu.VMEM(own_blocks.shape, jnp.bfloat16)
    probes, own_blocks, cross_blocks, level_perm = (
        pltpu.with_memory_space_constraint(a, pltpu.HBM)
        for a in (probes, own_blocks, cross_blocks, level_perm)
    )
    return pl.pallas_call(
        functools.partial(kernel, n_row, n_col, chunks),
        out_shape=jax.ShapeDtypeStruct((rows, depth), jnp.bfloat16),
        in_specs=[pl.BlockSpec(memory_space=pltpu.HBM)] * 4,
        out_specs=pl.BlockSpec(memory_space=pltpu.VMEM),
        scratch_shapes=[
            pltpu.VMEM((rows, depth), jnp.bfloat16),
            weights,
            weights,
            pltpu.VMEM(level_perm.shape, jnp.int32),
            weights,
            weights,
            pltpu.VMEM((LEVELS - 1, rows, depth), jnp.bfloat16),
            pltpu.VMEM((LEVELS, rows, depth), jnp.bfloat16),
            pltpu.VMEM((rows, depth), jnp.float32),
            pltpu.SemaphoreType.DMA((3,)),
            pltpu.SemaphoreType.DMA,
            pltpu.SemaphoreType.DMA((LEVELS, len(chunks))),
            pltpu.SemaphoreType.DMA((LEVELS, len(chunks))),
        ],
        compiler_params=pltpu.CompilerParams(
            collective_id=0, has_side_effects=True, vmem_limit_bytes=32 * 2**20
        ),
        cost_estimate=pl.CostEstimate(
            flops=24 * rows * depth * depth, bytes_accessed=8 * rows * depth * 2, transcendentals=0
        ),
    )(probes, own_blocks, cross_blocks, level_perm)


def solution(mesh):
    n_row, n_col = mesh.shape["row"], mesh.shape["col"]
    placed = (
        P(None, ("row", "col")),
        P(None, ("row", "col"), None),
        P(None, ("row", "col"), None),
        P(None, ("row", "col")),
    )
    return jax.shard_map(
        functools.partial(per_device, n_row, n_col),
        mesh=mesh,
        in_specs=placed,
        out_specs=P(None, ("row", "col")),
        check_vma=False,
    )
```

```python
import functools

import jax
import jax.numpy as jnp
from jax import lax
from jax.experimental import pallas as pl
from jax.experimental.pallas import tpu as pltpu
from jax.sharding import PartitionSpec as P

LEVELS = 3
BODY = 32
TAIL = (16, 16)
AHEAD = (6, 4)
LAG = 32
QUEUE = 96
JOIN = 64


def row_chunks(rows):
    sizes = list(TAIL) if rows > sum(TAIL) else []
    left = rows - sum(sizes)
    head = [BODY] * (left // BODY)
    if left % BODY:
        head.append(left % BODY)
    chunks, start = [], 0
    for size in head + sizes:
        chunks.append((start, size))
        start += size
    return chunks


def step_order(chunks):
    rows = sum(chunks[-1])
    steps, group = [], []
    for k, chunk in enumerate(chunks):
        due = sum(chunk)
        for level in range(LEVELS - 1):
            steps.append((due, level, (k,)))
            due += min(QUEUE, max(rows - due, 0)) + LAG
        group.append(k)
        if sum(chunks[j][1] for j in group) >= JOIN or len(chunks) - k in (1, 3):
            steps.append((due, LEVELS - 1, tuple(group)))
            group = []
    return [(level, ks) for _, level, ks in sorted(steps)]


def flip(index, distance):
    return index + distance - 2 * distance * lax.rem(lax.div(index, distance), 2)


def kernel(
    n_row, n_col, chunks,
    probes, own, cross, perm,
    out,
    mine, own_v, cross_v, perm_v, own_p, cross_p, panels, others, base,
    load_sem, perm_sem, send_sem, recv_sem,
):
    row, col = lax.axis_index("row"), lax.axis_index("col")
    partners = [
        (row, flip(col, n_col // 2)),
        (flip(row, n_row // 2), col),
        (row, flip(col, 1)),
    ]
    barrier = pltpu.get_barrier_semaphore()
    for partner in partners:
        pl.semaphore_signal(
            barrier, inc=1, device_id=partner, device_id_type=pl.DeviceIdType.MESH
        )
    loads = [
        pltpu.make_async_copy(perm, perm_v, perm_sem),
        pltpu.make_async_copy(own, own_v, load_sem.at[0]),
        pltpu.make_async_copy(cross, cross_v, load_sem.at[1]),
        pltpu.make_async_copy(probes, mine, load_sem.at[2]),
    ]
    for load in loads:
        load.start()
    pl.semaphore_wait(barrier, LEVELS)

    def send(level, k):
        start, size = chunks[k]
        rows = pl.ds(start, size)
        source = probes.at[rows] if level == 0 else panels.at[level - 1, rows]
        return pltpu.make_async_remote_copy(
            src_ref=source,
            dst_ref=others.at[level, rows],
            send_sem=send_sem.at[level, k],
            recv_sem=recv_sem.at[level, k],
            device_id=partners[level],
            device_id_type=pl.DeviceIdType.MESH,
        )

    copies = {}
    core = lax.rem(row, 2)
    for k in range(len(chunks)):
        copies[0, k] = send(0, k)
        if k < min(AHEAD):
            copies[0, k].start()
        elif k < max(AHEAD):
            pl.when(core == AHEAD.index(max(AHEAD)))(copies[0, k].start)

    for load in loads:
        load.wait()
    depth = own.shape[1]
    for level in range(LEVELS):
        index = lax.broadcasted_iota(jnp.int32, (depth, depth), 0)
        pick = jnp.where(index == perm_v[level : level + 1, :], 1.0, 0.0).astype(jnp.bfloat16)
        for source, target in ((own_v, own_p), (cross_v, cross_p)):
            moved = jnp.dot(source[level], pick, preferred_element_type=jnp.float32)
            target[level] = moved.astype(jnp.bfloat16)

    base[...] = jnp.dot(mine[...], own_p[0], preferred_element_type=jnp.float32)

    def step(level, ks):
        start, k = chunks[ks[0]][0], ks[-1]
        rows = pl.ds(start, sum(chunks[k]) - start)
        if level == 0:
            total = base[rows]
        else:
            total = jnp.dot(panels[level - 1, rows], own_p[level], preferred_element_type=jnp.float32)
        for j in ks:
            copies[level, j].wait_recv()
        total += jnp.dot(others[level, rows], cross_p[level], preferred_element_type=jnp.float32)
        result = total.astype(jnp.bfloat16)
        if level == LEVELS - 1:
            out[rows] = result
            return
        panels[level, rows] = result
        copies[level + 1, k] = send(level + 1, k)
        copies[level + 1, k].start()
        if level == 0:
            for which, ahead in enumerate(AHEAD):
                if k + ahead < len(chunks):
                    pl.when(core == which)(copies[0, k + ahead].start)

    for level, ks in step_order(chunks):
        step(level, ks)
    for copy in copies.values():
        copy.wait_send()


def per_device(n_row, n_col, probes, own_blocks, cross_blocks, level_perm):
    rows, depth = probes.shape
    chunks = row_chunks(rows)
    weights = pltpu.VMEM(own_blocks.shape, jnp.bfloat16)
    probes, own_blocks, cross_blocks, level_perm = (
        pltpu.with_memory_space_constraint(a, pltpu.HBM)
        for a in (probes, own_blocks, cross_blocks, level_perm)
    )
    return pl.pallas_call(
        functools.partial(kernel, n_row, n_col, chunks),
        out_shape=jax.ShapeDtypeStruct((rows, depth), jnp.bfloat16),
        in_specs=[pl.BlockSpec(memory_space=pltpu.HBM)] * 4,
        out_specs=pl.BlockSpec(memory_space=pltpu.VMEM),
        scratch_shapes=[
            pltpu.VMEM((rows, depth), jnp.bfloat16),
            weights,
            weights,
            pltpu.VMEM(level_perm.shape, jnp.int32),
            weights,
            weights,
            pltpu.VMEM((LEVELS - 1, rows, depth), jnp.bfloat16),
            pltpu.VMEM((LEVELS, rows, depth), jnp.bfloat16),
            pltpu.VMEM((rows, depth), jnp.float32),
            pltpu.SemaphoreType.DMA((3,)),
            pltpu.SemaphoreType.DMA,
            pltpu.SemaphoreType.DMA((LEVELS, len(chunks))),
            pltpu.SemaphoreType.DMA((LEVELS, len(chunks))),
        ],
        compiler_params=pltpu.CompilerParams(
            collective_id=0, has_side_effects=True, vmem_limit_bytes=32 * 2**20
        ),
        cost_estimate=pl.CostEstimate(
            flops=24 * rows * depth * depth, bytes_accessed=8 * rows * depth * 2, transcendentals=0
        ),
    )(probes, own_blocks, cross_blocks, level_perm)


def solution(mesh):
    n_row, n_col = mesh.shape["row"], mesh.shape["col"]
    placed = (
        P(None, ("row", "col")),
        P(None, ("row", "col"), None),
        P(None, ("row", "col"), None),
        P(None, ("row", "col")),
    )
    return jax.shard_map(
        functools.partial(per_device, n_row, n_col),
        mesh=mesh,
        in_specs=placed,
        out_specs=P(None, ("row", "col")),
        check_vma=False,
    )
```

```python
import functools

import jax
import jax.numpy as jnp
from jax import lax
from jax.experimental import pallas as pl
from jax.experimental.pallas import tpu as pltpu
from jax.sharding import PartitionSpec as P

LEVELS = 3
BODY = 32
TAIL = (16, 16)
AHEAD = (6, 4, 8, 6)
LAG = 32
QUEUE = 96
JOIN = 64


def row_chunks(rows):
    sizes = list(TAIL) if rows > sum(TAIL) else []
    left = rows - sum(sizes)
    head = [BODY] * (left // BODY)
    if left % BODY:
        head.append(left % BODY)
    chunks, start = [], 0
    for size in head + sizes:
        chunks.append((start, size))
        start += size
    return chunks


def step_order(chunks):
    rows = sum(chunks[-1])
    steps, group = [], []
    for k, chunk in enumerate(chunks):
        due = sum(chunk)
        for level in range(LEVELS - 1):
            steps.append((due, level, (k,)))
            due += min(QUEUE, max(rows - due, 0)) + LAG
        group.append(k)
        if sum(chunks[j][1] for j in group) >= JOIN or len(chunks) - k in (1, 3):
            steps.append((due, LEVELS - 1, tuple(group)))
            group = []
    return [(level, ks) for _, level, ks in sorted(steps)]


def flip(index, distance):
    return index + distance - 2 * distance * lax.rem(lax.div(index, distance), 2)


def kernel(
    n_row, n_col, chunks,
    probes, own, cross, perm,
    out,
    mine, own_v, cross_v, perm_v, own_p, cross_p, panels, others, base,
    load_sem, perm_sem, send_sem, recv_sem,
):
    row, col = lax.axis_index("row"), lax.axis_index("col")
    partners = [
        (row, flip(col, n_col // 2)),
        (flip(row, n_row // 2), col),
        (row, flip(col, 1)),
    ]
    barrier = pltpu.get_barrier_semaphore()
    for partner in partners:
        pl.semaphore_signal(
            barrier, inc=1, device_id=partner, device_id_type=pl.DeviceIdType.MESH
        )
    loads = [
        pltpu.make_async_copy(perm, perm_v, perm_sem),
        pltpu.make_async_copy(own, own_v, load_sem.at[0]),
        pltpu.make_async_copy(cross, cross_v, load_sem.at[1]),
        pltpu.make_async_copy(probes, mine, load_sem.at[2]),
    ]
    for load in loads:
        load.start()
    pl.semaphore_wait(barrier, LEVELS)

    def send(level, k):
        start, size = chunks[k]
        rows = pl.ds(start, size)
        source = probes.at[rows] if level == 0 else panels.at[level - 1, rows]
        return pltpu.make_async_remote_copy(
            src_ref=source,
            dst_ref=others.at[level, rows],
            send_sem=send_sem.at[level, k],
            recv_sem=recv_sem.at[level, k],
            device_id=partners[level],
            device_id_type=pl.DeviceIdType.MESH,
        )

    copies = {}
    place = 2 * lax.rem(lax.div(col, 2), 2) + lax.rem(row, 2)
    for k in range(len(chunks)):
        copies[0, k] = send(0, k)
        if k < min(AHEAD):
            copies[0, k].start()
            continue
        for which, ahead in enumerate(AHEAD):
            if k < ahead:
                pl.when(place == which)(copies[0, k].start)

    for load in loads:
        load.wait()
    depth = own.shape[1]
    for level in range(LEVELS):
        index = lax.broadcasted_iota(jnp.int32, (depth, depth), 0)
        pick = jnp.where(index == perm_v[level : level + 1, :], 1.0, 0.0).astype(jnp.bfloat16)
        for source, target in ((own_v, own_p), (cross_v, cross_p)):
            moved = jnp.dot(source[level], pick, preferred_element_type=jnp.float32)
            target[level] = moved.astype(jnp.bfloat16)

    base[...] = jnp.dot(mine[...], own_p[0], preferred_element_type=jnp.float32)

    def step(level, ks):
        start, k = chunks[ks[0]][0], ks[-1]
        rows = pl.ds(start, sum(chunks[k]) - start)
        if level == 0:
            total = base[rows]
        else:
            total = jnp.dot(panels[level - 1, rows], own_p[level], preferred_element_type=jnp.float32)
        for j in ks:
            copies[level, j].wait_recv()
        total += jnp.dot(others[level, rows], cross_p[level], preferred_element_type=jnp.float32)
        result = total.astype(jnp.bfloat16)
        if level == LEVELS - 1:
            out[rows] = result
            return
        panels[level, rows] = result
        copies[level + 1, k] = send(level + 1, k)
        copies[level + 1, k].start()
        if level == 0:
            for which, ahead in enumerate(AHEAD):
                if k + ahead < len(chunks):
                    pl.when(place == which)(copies[0, k + ahead].start)

    for level, ks in step_order(chunks):
        step(level, ks)
    for copy in copies.values():
        copy.wait_send()


def per_device(n_row, n_col, probes, own_blocks, cross_blocks, level_perm):
    rows, depth = probes.shape
    chunks = row_chunks(rows)
    weights = pltpu.VMEM(own_blocks.shape, jnp.bfloat16)
    probes, own_blocks, cross_blocks, level_perm = (
        pltpu.with_memory_space_constraint(a, pltpu.HBM)
        for a in (probes, own_blocks, cross_blocks, level_perm)
    )
    return pl.pallas_call(
        functools.partial(kernel, n_row, n_col, chunks),
        out_shape=jax.ShapeDtypeStruct((rows, depth), jnp.bfloat16),
        in_specs=[pl.BlockSpec(memory_space=pltpu.HBM)] * 4,
        out_specs=pl.BlockSpec(memory_space=pltpu.VMEM),
        scratch_shapes=[
            pltpu.VMEM((rows, depth), jnp.bfloat16),
            weights,
            weights,
            pltpu.VMEM(level_perm.shape, jnp.int32),
            weights,
            weights,
            pltpu.VMEM((LEVELS - 1, rows, depth), jnp.bfloat16),
            pltpu.VMEM((LEVELS, rows, depth), jnp.bfloat16),
            pltpu.VMEM((rows, depth), jnp.float32),
            pltpu.SemaphoreType.DMA((3,)),
            pltpu.SemaphoreType.DMA,
            pltpu.SemaphoreType.DMA((LEVELS, len(chunks))),
            pltpu.SemaphoreType.DMA((LEVELS, len(chunks))),
        ],
        compiler_params=pltpu.CompilerParams(
            collective_id=0, has_side_effects=True, vmem_limit_bytes=32 * 2**20
        ),
        cost_estimate=pl.CostEstimate(
            flops=24 * rows * depth * depth, bytes_accessed=8 * rows * depth * 2, transcendentals=0
        ),
    )(probes, own_blocks, cross_blocks, level_perm)


def solution(mesh):
    n_row, n_col = mesh.shape["row"], mesh.shape["col"]
    placed = (
        P(None, ("row", "col")),
        P(None, ("row", "col"), None),
        P(None, ("row", "col"), None),
        P(None, ("row", "col")),
    )
    return jax.shard_map(
        functools.partial(per_device, n_row, n_col),
        mesh=mesh,
        in_specs=placed,
        out_specs=P(None, ("row", "col")),
        check_vma=False,
    )
```
